32 devices in a mesh: grid: 16 (over z, x, core), layer: 2 (over y).
Axes of the slice: x: 2, y: 2, z: 4, core: 2. Of those that a mesh axis runs over, the one named last changes fastest.
Arguments:
- x_tiles: bfloat16 [16, 512, 512], P('grid'), may hold values from -1.03 to 1.03, as said below
- pattern: int32 [16, 8, 8], P('grid'), may hold values from 0 to 1, as said below
Outputs:
- signed: bfloat16 [16, 128, 512], P('grid', 'layer')
The draws below stay inside these ranges and needn't reach their ends.
Inputs may be any that keep to these rules, and one draw needn't show every extreme that they name: `x_tiles`: tile (j, i) is the transpose of tile (i, j). symmetric: the block pattern of the whole matrix is its own transpose, and every diagonal block is kept.
All inputs are finite; a program needn't handle non-finite values.
Results may differ from the reference program's by a relative error of at most 0.013.
Values may be sent and summed in bfloat16 or wider, within the bound.
A program may use at most 64 MiB of HBM per device.

```python
import math
import jax
import jax.numpy as jnp

BLOCK = 64
TILE_BLK = 8
SIDE = 4
TILE = 512
SLAB = 128
N_GRID = 16


def draw_x_tiles(key, part):
    order = SIDE * TILE
    first, second, third = jax.random.split(key, 3)
    spread = 0.6 / math.sqrt(64.0 * 13.0)
    noise = jnp.clip(jax.random.normal(first, (order, order), jnp.float32), -4.0, 4.0) * spread
    mirrored = (noise + noise.T) * 0.7071
    magnitude = jax.random.uniform(second, (order,), jnp.float32, 0.4, 0.9)
    signs = jnp.where(jax.random.bernoulli(third, 0.5, (order,)), 1.0, -1.0)
    whole = mirrored + jnp.diag(magnitude * signs)
    whole = whole.reshape(SIDE, TILE, SIDE, TILE).transpose(0, 2, 1, 3)
    return whole.reshape(SIDE * SIDE, TILE, TILE).astype(jnp.bfloat16)


def draw_pattern(key, part):
    count = SIDE * TILE_BLK
    first, second, third = jax.random.split(key, 3)
    reach = jax.random.randint(first, (count,), 1, 9)
    places = jnp.arange(count)
    apart = jnp.abs(places[:, None] - places[None, :])
    apart = jnp.minimum(apart, count - apart)
    inside = apart <= jnp.maximum(reach[:, None], reach[None, :])
    extra = jax.random.randint(second, (count, count), 0, 512)
    extra = jnp.where(places[:, None] <= places[None, :], extra, extra.T)
    whole = jnp.where(inside | (extra == 0), 1, 0).astype(jnp.int32)
    shuffle = jax.random.permutation(third, count).astype(jnp.int32)
    whole = jnp.take(jnp.take(whole, shuffle, axis=0), shuffle, axis=1)
    whole = whole.reshape(SIDE, TILE_BLK, SIDE, TILE_BLK).transpose(0, 2, 1, 3)
    return whole.reshape(SIDE * SIDE, TILE_BLK, TILE_BLK)


def setup_inputs(seed: int = 0) -> dict:
    seeds = jax.random.split(jax.random.key(seed), 3)
    return {
        "x_tiles": draw_x_tiles(jax.random.fold_in(seeds[2], 71), 0),
        "pattern": draw_pattern(jax.random.fold_in(seeds[2], 71), 0),
    }


def reference(x_tiles, pattern):
    order = SIDE * TILE
    mask = jnp.broadcast_to(pattern[:, :, None, :, None], (N_GRID, TILE_BLK, BLOCK, TILE_BLK, BLOCK))
    mask = mask.reshape(N_GRID, TILE, TILE).astype(jnp.bfloat16)
    tiles = x_tiles * mask
    matrix = tiles.reshape(SIDE, SIDE, TILE, TILE).transpose(0, 2, 1, 3).reshape(order, order)
    slab = matrix.reshape(SIDE, TILE, order)[:, :SLAB, :].reshape(SIDE * SLAB, order)
    squared = jnp.dot(slab, matrix, preferred_element_type=jnp.float32).astype(jnp.bfloat16)
    cubed = jnp.dot(squared, matrix, preferred_element_type=jnp.float32)
    signed = (1.5 * slab.astype(jnp.float32) - 0.5 * cubed).astype(jnp.bfloat16)
    return signed.reshape(SIDE, SLAB, SIDE, TILE).transpose(0, 2, 1, 3).reshape(N_GRID, SLAB, TILE)
```

```python
import functools
import math

import jax
import jax.numpy as jnp
from jax import lax
from jax.experimental import pallas as pl
from jax.experimental.pallas import tpu as pltpu
from jax.sharding import PartitionSpec as P

SLAB = 128
MESH = pl.DeviceIdType.MESH


def flip(number, level):
    step = 1 << level
    return number + (1 - 2 * (number // step % 2)) * step


def nearest(n, a, k):
    inner = jnp.minimum(a, n - 1 - a)
    around = a + (k + 1) // 2 if k % 2 else a - k // 2
    beyond = jnp.where(2 * a < n, k, n - 1 - k)
    return jnp.where(k <= 2 * inner, around, beyond)


def kernel(n, x_ref, pattern_ref, out_ref, own_x, x, m, s, kept, core_out, core_in, far_out, far_in,
           squared, cubed, back_out, back_in, load_sem, s_send, s_recv, core_send, core_recv,
           far_send, far_recv, pair_send, pair_recv, back_send, back_recv):
    position = lax.axis_index("grid")
    a, b = position // n, position % n
    layer = lax.axis_index("layer")
    bits = n.bit_length() - 1
    rows, width = own_x.shape
    half = rows // 2
    blocks = pattern_ref.shape[1]
    span = width // blocks
    core = b % 2
    line = [nearest(n, a, k) for k in range(n)]
    column = [{"grid": line[k] * n + b} for k in range(n)]
    partner = [{"grid": a * n + flip(b, level)} for level in range(bits)]

    barrier = pltpu.get_barrier_semaphore()
    for peer in column[1:] + partner:
        pl.semaphore_signal(barrier, inc=1, device_id=peer, device_id_type=MESH)
    load_own = pltpu.make_async_copy(
        x_ref.at[0, pl.ds(pl.multiple_of(layer * rows, rows), rows), :], own_x, load_sem.at[0])
    load_own.start()
    load_all = pltpu.make_async_copy(x_ref.at[0], x, load_sem.at[1])
    load_all.start()

    def inside(place, block):
        return ((place >= block * span) & (place < (block + 1) * span)).astype(jnp.float32)

    def iota(shape, dim):
        return lax.broadcasted_iota(jnp.int32, shape, dim)

    spread = inside(iota((blocks, width), 1), iota((blocks, width), 0))
    across = jnp.dot(pattern_ref[0].astype(jnp.float32), spread, preferred_element_type=jnp.float32)
    down = inside(iota((rows, blocks), 0) + layer * rows, iota((rows, blocks), 1))
    own_mask = jnp.dot(down, across, preferred_element_type=jnp.float32)
    load_own.wait()
    s[a] = own_x[...] * own_mask.astype(jnp.bfloat16)
    pl.semaphore_wait(barrier, n - 1 + bits)

    def s_copy(k, slot):
        return pltpu.make_async_remote_copy(
            src_ref=s.at[slot], dst_ref=s.at[slot], send_sem=s_send.at[k], recv_sem=s_recv.at[slot],
            device_id=column[k], device_id_type=MESH)

    def core_copy(k):
        return pltpu.make_async_remote_copy(
            src_ref=core_out.at[k], dst_ref=core_in.at[k], send_sem=core_send.at[k],
            recv_sem=core_recv.at[k], device_id=partner[0], device_id_type=MESH)

    def far_copy(k, level):
        return pltpu.make_async_remote_copy(
            src_ref=far_out.at[level - 1, k], dst_ref=far_in.at[level - 1, k],
            send_sem=far_send.at[level - 1, k], recv_sem=far_recv.at[level - 1, k],
            device_id=partner[level], device_id_type=MESH)

    def pair_copy(k, which):
        return pltpu.make_async_remote_copy(
            src_ref=squared.at[k, which], dst_ref=squared.at[k, which], send_sem=pair_send.at[k],
            recv_sem=pair_recv.at[k], device_id=partner[0], device_id_type=MESH)

    def back_copy(k, slot):
        return pltpu.make_async_remote_copy(
            src_ref=back_out.at[k], dst_ref=back_in.at[slot], send_sem=back_send.at[k],
            recv_sem=back_recv.at[slot], device_id=column[k], device_id_type=MESH)

    for k in range(1, n):
        s_copy(k, a).start()
    load_all.wait()
    for block in range(blocks):
        part = pl.ds(block * span, span)
        m[part, :] = x[part, :] * across[block:block + 1, :].astype(jnp.bfloat16)

    def first(k):
        if k > 0:
            s_copy(k, line[k]).wait_recv()
        product = lax.dot_general(
            s[line[k]], m[...], (((1,), (1,)), ((), ())), preferred_element_type=jnp.float32)
        low, high = product[:half], product[half:]
        core_out[k] = jnp.where(core == 0, high, low).astype(jnp.bfloat16)
        core_copy(k).start()
        kept[k] = jnp.where(core == 0, low, high)

    def pair_sum(k):
        core_copy(k).wait_recv()
        total = kept[k] + core_in[k].astype(jnp.float32)
        kept[k] = total
        far_out[0, k] = total.astype(jnp.bfloat16)
        far_copy(k, 1).start()

    def row_sum(k):
        for level in range(1, bits):
            far_copy(k, level).wait_recv()
            total = kept[k] + far_in[level - 1, k].astype(jnp.float32)
            if level + 1 < bits:
                kept[k] = total
                far_out[level, k] = total.astype(jnp.bfloat16)
                far_copy(k, level + 1).start()
        squared[k, core] = total.astype(jnp.bfloat16)
        pair_copy(k, core).start()

    def second(k):
        pair_copy(k, 1 - core).wait_recv()
        left = squared[k].reshape(rows, width)
        product = jnp.dot(left, m[...], preferred_element_type=jnp.float32)
        if k == 0:
            cubed[...] = product
        else:
            back_out[k] = product.astype(jnp.bfloat16)
            back_copy(k, a).start()

    stages = [second, row_sum, pair_sum, first]
    for turn in range(n + 3):
        for late, stage in enumerate(stages):
            k = turn - 3 + late
            if 0 <= k < n:
                stage(k)

    total = cubed[...]
    for k in range(1, n):
        back_copy(k, line[k]).wait_recv()
        total = total + back_in[line[k]].astype(jnp.float32)
    out_ref[0] = (1.5 * s[a].astype(jnp.float32) - 0.5 * total).astype(jnp.bfloat16)
    for k in range(n):
        core_copy(k).wait_send()
        for level in range(1, bits):
            far_copy(k, level).wait_send()
        pair_copy(k, core).wait_send()
        if k > 0:
            s_copy(k, a).wait_send()
            back_copy(k, a).wait_send()


def shards(x_tiles, pattern):
    n = math.isqrt(lax.axis_size("grid"))
    bits = n.bit_length() - 1
    rows = SLAB // lax.axis_size("layer")
    width = x_tiles.shape[2]
    half = rows // 2
    bf16, f32 = jnp.bfloat16, jnp.float32
    dma = pltpu.SemaphoreType.DMA
    return pl.pallas_call(
        functools.partial(kernel, n),
        out_shape=jax.ShapeDtypeStruct((1, rows, width), bf16),
        in_specs=[pl.BlockSpec(memory_space=pl.ANY), pl.BlockSpec(memory_space=pltpu.VMEM)],
        out_specs=pl.BlockSpec(memory_space=pltpu.VMEM),
        scratch_shapes=[
            pltpu.VMEM((rows, width), bf16),
            pltpu.VMEM((width, width), bf16),
            pltpu.VMEM((width, width), bf16),
            pltpu.VMEM((n, rows, width), bf16),
            pltpu.VMEM((n, half, width), f32),
            pltpu.VMEM((n, half, width), bf16),
            pltpu.VMEM((n, half, width), bf16),
            pltpu.VMEM((bits - 1, n, half, width), bf16),
            pltpu.VMEM((bits - 1, n, half, width), bf16),
            pltpu.VMEM((n, 2, half, width), bf16),
            pltpu.VMEM((rows, width), f32),
            pltpu.VMEM((n, rows, width), bf16),
            pltpu.VMEM((n, rows, width), bf16),
            dma((2,)),
            dma((n,)), dma((n,)),
            dma((n,)), dma((n,)),
            dma((bits - 1, n)), dma((bits - 1, n)),
            dma((n,)), dma((n,)),
            dma((n,)), dma((n,)),
        ],
        compiler_params=pltpu.CompilerParams(
            collective_id=0, has_side_effects=True, vmem_limit_bytes=40 * 1024 * 1024),
        cost_estimate=pl.CostEstimate(
            flops=4 * n * rows * width * width, bytes_accessed=2 * width * width, transcendentals=0),
    )(x_tiles, pattern)


def solution(mesh):
    in_specs = (P("grid", None, None), P("grid", None, None))
    out_specs = P("grid", "layer", None)
    return jax.shard_map(shards, mesh=mesh, in_specs=in_specs, out_specs=out_specs, check_vma=False)
```

```python
import functools
import math

import jax
import jax.numpy as jnp
from jax import lax
from jax.experimental import pallas as pl
from jax.experimental.pallas import tpu as pltpu
from jax.sharding import PartitionSpec as P

SLAB = 128
MESH = pl.DeviceIdType.MESH


def flip(number, level):
    step = 1 << level
    return number + (1 - 2 * (number // step % 2)) * step


def xor(number, mask):
    for level in range(mask.bit_length()):
        if mask >> level & 1:
            number = flip(number, level)
    return number


def kernel(n, x_ref, pattern_ref, out_ref, pattern, own_x, x, m, s, kept, core_out, core_in, far_out,
           far_in, cubed, back_out, back_in, load_sem, s_send, s_recv, core_send, core_recv,
           far_send, far_recv, back_send, back_recv):
    position = lax.axis_index("grid")
    a, b = position // n, position % n
    layer = lax.axis_index("layer")
    bits = n.bit_length() - 1
    rows, width = own_x.shape
    half = rows // 2
    blocks = pattern.shape[1]
    span = width // blocks
    core = b % 2
    order = [0, 1] + [k ^ 1 for k in range(2, n)]
    line = [xor(a, k) for k in order]
    column = [{"grid": line[k] * n + b} for k in range(n)]
    partner = [a * n + flip(b, level) for level in range(bits)]
    across_chips = [(level, other) for level in range(1, bits) for other in range(2)]
    row = [{"grid": partner[0]}]
    for level, other in across_chips:
        row.append({"grid": partner[level] if other == 0 else flip(partner[level], 0)})

    barrier = pltpu.get_barrier_semaphore()
    for peer in column[1:] + row:
        pl.semaphore_signal(barrier, inc=1, device_id=peer, device_id_type=MESH)
    load_pattern = pltpu.make_async_copy(pattern_ref, pattern, load_sem.at[2])
    load_pattern.start()
    load_own = pltpu.make_async_copy(
        x_ref.at[0, pl.ds(pl.multiple_of(layer * rows, rows), rows), :], own_x, load_sem.at[0])
    load_own.start()
    load_all = pltpu.make_async_copy(x_ref.at[0], x, load_sem.at[1])
    load_all.start()

    def inside(place, block):
        return ((place >= block * span) & (place < (block + 1) * span)).astype(jnp.float32)

    def iota(shape, dim):
        return lax.broadcasted_iota(jnp.int32, shape, dim)

    spread = inside(iota((blocks, width), 1), iota((blocks, width), 0))
    load_pattern.wait()
    across = jnp.dot(pattern[0].astype(jnp.float32), spread, preferred_element_type=jnp.float32)
    down = inside(iota((rows, blocks), 0) + layer * rows, iota((rows, blocks), 1))
    own_mask = jnp.dot(down, across, preferred_element_type=jnp.float32)
    load_own.wait()
    s[a] = own_x[...] * own_mask.astype(jnp.bfloat16)
    pl.semaphore_wait(barrier, n - 1 + len(row))

    def s_copy(k, slot):
        return pltpu.make_async_remote_copy(
            src_ref=s.at[slot], dst_ref=s.at[slot], send_sem=s_send.at[k], recv_sem=s_recv.at[slot],
            device_id=column[k], device_id_type=MESH)

    def core_copy(k):
        return pltpu.make_async_remote_copy(
            src_ref=core_out.at[k], dst_ref=core_in.at[k], send_sem=core_send.at[k],
            recv_sem=core_recv.at[k], device_id=row[0], device_id_type=MESH)

    def far_copy(k, level, other, which):
        return pltpu.make_async_remote_copy(
            src_ref=far_out.at[level - 1, k], dst_ref=far_in.at[level - 1, k, which],
            send_sem=far_send.at[level - 1, k, other], recv_sem=far_recv.at[level - 1, k, which],
            device_id=row[2 * level - 1 + other], device_id_type=MESH)

    def back_copy(k, slot):
        return pltpu.make_async_remote_copy(
            src_ref=back_out.at[k], dst_ref=back_in.at[slot], send_sem=back_send.at[k],
            recv_sem=back_recv.at[slot], device_id=column[k], device_id_type=MESH)

    for k in range(1, n):
        s_copy(k, a).start()
    load_all.wait()
    for block in range(blocks):
        part = pl.ds(block * span, span)
        m[part, :] = x[part, :] * across[block:block + 1, :].astype(jnp.bfloat16)

    def first(k):
        if k > 0:
            s_copy(k, line[k]).wait_recv()
        product = lax.dot_general(
            s[line[k]], m[...], (((1,), (1,)), ((), ())), preferred_element_type=jnp.float32)
        core_out[k] = product.astype(jnp.bfloat16)
        core_copy(k).start()
        kept[k] = product

    def send_half(k, level, total):
        far_out[level - 1, k] = jnp.where(core == 0, total[:half], total[half:]).astype(jnp.bfloat16)
        for other in range(2):
            far_copy(k, level, other, core).start()

    def pair_sum(k):
        core_copy(k).wait_recv()
        total = kept[k] + core_in[k].astype(jnp.float32)
        kept[k] = total
        send_half(k, 1, total)

    def second(k):
        total = kept[k]
        for level in range(1, bits):
            for which in range(2):
                far_copy(k, level, 0, which).wait_recv()
            total = total + far_in[level - 1, k].reshape(rows, width).astype(jnp.float32)
            if level + 1 < bits:
                send_half(k, level + 1, total)
        product = jnp.dot(total.astype(jnp.bfloat16), m[...], preferred_element_type=jnp.float32)
        if k == 0:
            cubed[...] = product
        else:
            back_out[k] = product.astype(jnp.bfloat16)
            back_copy(k, a).start()

    for k in range(n):
        first(k)
        pair_sum(k)
    for k in range(n):
        second(k)

    total = cubed[...]
    for k in range(1, n):
        back_copy(k, line[k]).wait_recv()
        total = total + back_in[line[k]].astype(jnp.float32)
    out_ref[0] = (1.5 * s[a].astype(jnp.float32) - 0.5 * total).astype(jnp.bfloat16)
    for k in range(n):
        core_copy(k).wait_send()
        for level, other in across_chips:
            far_copy(k, level, other, core).wait_send()
        if k > 0:
            s_copy(k, a).wait_send()
            back_copy(k, a).wait_send()


def shards(x_tiles, pattern):
    n = math.isqrt(lax.axis_size("grid"))
    bits = n.bit_length() - 1
    rows = SLAB // lax.axis_size("layer")
    width = x_tiles.shape[2]
    half = rows // 2
    bf16, f32 = jnp.bfloat16, jnp.float32
    dma = pltpu.SemaphoreType.DMA
    return pl.pallas_call(
        functools.partial(kernel, n),
        out_shape=jax.ShapeDtypeStruct((1, rows, width), bf16),
        in_specs=[pl.BlockSpec(memory_space=pltpu.HBM)] * 2,
        out_specs=pl.BlockSpec(memory_space=pltpu.VMEM),
        scratch_shapes=[
            pltpu.VMEM(pattern.shape, pattern.dtype),
            pltpu.VMEM((rows, width), bf16),
            pltpu.VMEM((width, width), bf16),
            pltpu.VMEM((width, width), bf16),
            pltpu.VMEM((n, rows, width), bf16),
            pltpu.VMEM((n, rows, width), f32),
            pltpu.VMEM((n, rows, width), bf16),
            pltpu.VMEM((n, rows, width), bf16),
            pltpu.VMEM((bits - 1, n, half, width), bf16),
            pltpu.VMEM((bits - 1, n, 2, half, width), bf16),
            pltpu.VMEM((rows, width), f32),
            pltpu.VMEM((n, rows, width), bf16),
            pltpu.VMEM((n, rows, width), bf16),
            dma((3,)),
            dma((n,)), dma((n,)),
            dma((n,)), dma((n,)),
            dma((bits - 1, n, 2)), dma((bits - 1, n, 2)),
            dma((n,)), dma((n,)),
        ],
        compiler_params=pltpu.CompilerParams(
            collective_id=0, has_side_effects=True, vmem_limit_bytes=63 * 1024 * 1024),
        cost_estimate=pl.CostEstimate(
            flops=4 * n * rows * width * width, bytes_accessed=2 * width * width, transcendentals=0),
    )(x_tiles, pattern)


def solution(mesh):
    in_specs = (P("grid", None, None), P("grid", None, None))
    out_specs = P("grid", "layer", None)
    return jax.shard_map(shards, mesh=mesh, in_specs=in_specs, out_specs=out_specs, check_vma=False)
```

```python
import functools
import math

import jax
import jax.numpy as jnp
from jax import lax
from jax.experimental import pallas as pl
from jax.experimental.pallas import tpu as pltpu
from jax.sharding import PartitionSpec as P

SLAB = 128
MESH = pl.DeviceIdType.MESH


def flip(number, level):
    step = 1 << level
    return number + (1 - 2 * (number // step % 2)) * step


def xor(number, mask):
    for level in range(mask.bit_length()):
        if mask >> level & 1:
            number = flip(number, level)
    return number


def kernel(n, x_ref, pattern_ref, out_ref, pattern, own_x, x, m, s, kept, core_out, core_in, far_out,
           far_in, cubed, back_out, back_in, load_sem, s_send, s_recv, core_send, core_recv,
           far_send, far_recv, back_send, back_recv):
    position = lax.axis_index("grid")
    a, b = position // n, position % n
    layer = lax.axis_index("layer")
    bits = n.bit_length() - 1
    rows, width = own_x.shape
    half = rows // 2
    blocks = pattern.shape[1]
    span = width // blocks
    core = b % 2
    line = [xor(a, k) for k in range(n)]
    column = [{"grid": line[k] * n + b} for k in range(n)]
    partner = [a * n + flip(b, level) for level in range(bits)]
    across_chips = [(level, other) for level in range(1, bits) for other in range(2)]
    row = [{"grid": partner[0]}]
    for level, other in across_chips:
        row.append({"grid": partner[level] if other == 0 else flip(partner[level], 0)})

    barrier = pltpu.get_barrier_semaphore()
    for peer in column[1:] + row:
        pl.semaphore_signal(barrier, inc=1, device_id=peer, device_id_type=MESH)
    load_pattern = pltpu.make_async_copy(pattern_ref, pattern, load_sem.at[2])
    load_pattern.start()
    load_own = pltpu.make_async_copy(
        x_ref.at[0, pl.ds(pl.multiple_of(layer * rows, rows), rows), :], own_x, load_sem.at[0])
    load_own.start()
    load_all = pltpu.make_async_copy(x_ref.at[0], x, load_sem.at[1])
    load_all.start()

    def inside(place, block):
        return ((place >= block * span) & (place < (block + 1) * span)).astype(jnp.float32)

    def iota(shape, dim):
        return lax.broadcasted_iota(jnp.int32, shape, dim)

    spread = inside(iota((blocks, width), 1), iota((blocks, width), 0))
    load_pattern.wait()
    across = jnp.dot(pattern[0].astype(jnp.float32), spread, preferred_element_type=jnp.float32)
    down = inside(iota((rows, blocks), 0) + layer * rows, iota((rows, blocks), 1))
    own_mask = jnp.dot(down, across, preferred_element_type=jnp.float32)
    load_own.wait()
    s[a] = own_x[...] * own_mask.astype(jnp.bfloat16)
    pl.semaphore_wait(barrier, n - 1 + len(row))

    def s_copy(k, slot):
        return pltpu.make_async_remote_copy(
            src_ref=s.at[slot], dst_ref=s.at[slot], send_sem=s_send.at[k], recv_sem=s_recv.at[slot],
            device_id=column[k], device_id_type=MESH)

    def core_copy(k):
        return pltpu.make_async_remote_copy(
            src_ref=core_out.at[k], dst_ref=core_in.at[k], send_sem=core_send.at[k],
            recv_sem=core_recv.at[k], device_id=row[0], device_id_type=MESH)

    def far_copy(k, level, other, which):
        return pltpu.make_async_remote_copy(
            src_ref=far_out.at[level - 1, k], dst_ref=far_in.at[level - 1, k, which],
            send_sem=far_send.at[level - 1, k, other], recv_sem=far_recv.at[level - 1, k, which],
            device_id=row[2 * level - 1 + other], device_id_type=MESH)

    def back_copy(k, slot):
        return pltpu.make_async_remote_copy(
            src_ref=back_out.at[k], dst_ref=back_in.at[slot], send_sem=back_send.at[k],
            recv_sem=back_recv.at[slot], device_id=column[k], device_id_type=MESH)

    for k in range(1, n):
        s_copy(k, a).start()
    load_all.wait()
    for block in range(blocks):
        part = pl.ds(block * span, span)
        m[part, :] = x[part, :] * across[block:block + 1, :].astype(jnp.bfloat16)

    def first(k):
        if k > 0:
            s_copy(k, line[k]).wait_recv()
        product = lax.dot_general(
            s[line[k]], m[...], (((1,), (1,)), ((), ())), preferred_element_type=jnp.float32)
        core_out[k] = product.astype(jnp.bfloat16)
        core_copy(k).start()
        kept[k] = product

    def send_half(k, level, total):
        far_out[level - 1, k] = jnp.where(core == 0, total[:half], total[half:]).astype(jnp.bfloat16)
        for other in range(2):
            far_copy(k, level, other, core).start()

    def pair_sum(k):
        core_copy(k).wait_recv()
        total = kept[k] + core_in[k].astype(jnp.float32)
        kept[k] = total
        send_half(k, 1, total)

    def second(k):
        total = kept[k]
        for level in range(1, bits):
            for which in range(2):
                far_copy(k, level, 0, which).wait_recv()
            total = total + far_in[level - 1, k].reshape(rows, width).astype(jnp.float32)
            if level + 1 < bits:
                send_half(k, level + 1, total)
        product = jnp.dot(total.astype(jnp.bfloat16), m[...], preferred_element_type=jnp.float32)
        if k == 0:
            cubed[...] = product
        else:
            back_out[k] = product.astype(jnp.bfloat16)
            back_copy(k, a).start()

    for k in range(n):
        first(k)
        pair_sum(k)
    for k in [*range(1, n - 1), 0, n - 1]:
        second(k)

    total = cubed[...]
    for k in range(1, n):
        back_copy(k, line[k]).wait_recv()
        total = total + back_in[line[k]].astype(jnp.float32)
    out_ref[0] = (1.5 * s[a].astype(jnp.float32) - 0.5 * total).astype(jnp.bfloat16)
    for k in range(n):
        core_copy(k).wait_send()
        for level, other in across_chips:
            far_copy(k, level, other, core).wait_send()
        if k > 0:
            s_copy(k, a).wait_send()
            back_copy(k, a).wait_send()


def shards(x_tiles, pattern):
    n = math.isqrt(lax.axis_size("grid"))
    bits = n.bit_length() - 1
    rows = SLAB // lax.axis_size("layer")
    width = x_tiles.shape[2]
    half = rows // 2
    bf16, f32 = jnp.bfloat16, jnp.float32
    dma = pltpu.SemaphoreType.DMA
    return pl.pallas_call(
        functools.partial(kernel, n),
        out_shape=jax.ShapeDtypeStruct((1, rows, width), bf16),
        in_specs=[pl.BlockSpec(memory_space=pltpu.HBM)] * 2,
        out_specs=pl.BlockSpec(memory_space=pltpu.VMEM),
        scratch_shapes=[
            pltpu.VMEM(pattern.shape, pattern.dtype),
            pltpu.VMEM((rows, width), bf16),
            pltpu.VMEM((width, width), bf16),
            pltpu.VMEM((width, width), bf16),
            pltpu.VMEM((n, rows, width), bf16),
            pltpu.VMEM((n, rows, width), f32),
            pltpu.VMEM((n, rows, width), bf16),
            pltpu.VMEM((n, rows, width), bf16),
            pltpu.VMEM((bits - 1, n, half, width), bf16),
            pltpu.VMEM((bits - 1, n, 2, half, width), bf16),
            pltpu.VMEM((rows, width), f32),
            pltpu.VMEM((n, rows, width), bf16),
            pltpu.VMEM((n, rows, width), bf16),
            dma((3,)),
            dma((n,)), dma((n,)),
            dma((n,)), dma((n,)),
            dma((bits - 1, n, 2)), dma((bits - 1, n, 2)),
            dma((n,)), dma((n,)),
        ],
        compiler_params=pltpu.CompilerParams(
            collective_id=0, has_side_effects=True, vmem_limit_bytes=63 * 1024 * 1024),
        cost_estimate=pl.CostEstimate(
            flops=4 * n * rows * width * width, bytes_accessed=2 * width * width, transcendentals=0),
    )(x_tiles, pattern)


def solution(mesh):
    in_specs = (P("grid", None, None), P("grid", None, None))
    out_specs = P("grid", "layer", None)
    return jax.shard_map(shards, mesh=mesh, in_specs=in_specs, out_specs=out_specs, check_vma=False)
```
